```python
import math
import jax
import jax.numpy as jnp
from jax import lax

D = 1152
HEADS = 16
HEAD_DIM = 72
FF = 4304
SEQ = 729
LAYERS = 2
STEP = 10
IMAGES = 16
SEQ_PAD = 732


def draw_vector_params(key, part):
    key = jax.random.fold_in(key, 7)
    gain_key, shift_key = jax.random.split(key)
    gain_rows = 1.0 + 0.15 * jax.random.truncated_normal(gain_key, -3.0, 3.0, (LAYERS, 2, D), jnp.float32)
    shifts = 0.3 * jax.random.truncated_normal(shift_key, -3.0, 3.0, (LAYERS, 4, D), jnp.float32)
    return jnp.stack([gain_rows[:, 0], shifts[:, 0], gain_rows[:, 1], shifts[:, 1], shifts[:, 2], shifts[:, 3]], axis=1)


def block_levels(key, shape, pieces, least, top_value):
    gain = 1.0
    for position, parts in pieces:
        draws = jax.random.uniform(jax.random.fold_in(jax.random.fold_in(key, 6), position), (parts,), jnp.float32, least / len(pieces), top_value / len(pieces))
        gain = gain * jnp.repeat(jnp.exp(draws), shape[position] // parts).reshape((-1,) + (1,) * (len(shape) - 1 - position))
    return gain


def noise(key, shape, spread, most, shards=(), held_as=jnp.bfloat16):
    gain = block_levels(key, shape, shards, -0.22, 0.18) if shards else 1.0
    result = jax.random.normal(key, shape, jnp.float32) * spread * gain
    return jnp.minimum(jnp.maximum(result, -most), most).astype(held_as)


def setup_inputs(seed: int = 0) -> dict:
    key_of = jax.random.split(jax.random.key(seed), 24)
    return {
        "stream_in": noise(key_of[0], (IMAGES, SEQ_PAD, D), 1.0, 6.0, ((0, 8), (1, 4)), jnp.float32),
        "cotangent": noise(key_of[1], (IMAGES, SEQ_PAD, D), 1.0, 6.0, ((0, 8), (1, 4)), jnp.float32),
        "attention_input": noise(key_of[2], (LAYERS, D, 3, D), D ** -0.5, 0.1875, ((1, 8), (3, 4)), jnp.float32),
        "attention_output": noise(key_of[3], (LAYERS, D, D), (D * 4 // SEQ) ** -0.5, 2.5, ((1, 4), (2, 8)), jnp.float32),
        "expand_weight": noise(key_of[4], (LAYERS, D, FF), D ** -0.5, 0.1875, ((1, 8), (2, 4)), jnp.float32),
        "reduce_weight": noise(key_of[5], (LAYERS, FF, D), FF ** -0.5, 0.09375, ((1, 4), (2, 8)), jnp.float32),
        "head_bias": noise(key_of[6], (LAYERS, 2, D), 0.5, 3.0, ((2, 4),), jnp.float32),
        "expand_bias": noise(key_of[7], (LAYERS, FF), 0.5, 3.0, ((1, 4),), jnp.float32),
        "vector_params": draw_vector_params(jax.random.fold_in(key_of[23], 71), 0),
        "attention_input_mean": noise(key_of[9], (LAYERS, D, 3, D), (0.11 * (IMAGES * SEQ) ** 0.5), 64.0, ((1, 8), (3, 4)), jnp.float32),
        "attention_input_square": jnp.clip(jnp.exp(math.log(46.656) - 1.3862944 * jax.random.uniform(key_of[10], (LAYERS, D, 3, D), jnp.float32) ** block_levels(key_of[10], (LAYERS, D, 3, D), ((1, 8), (3, 4)), -0.2, 0.2)), 11.664, 46.656),
        "attention_output_mean": noise(key_of[11], (LAYERS, D, D), (0.0077 * (IMAGES * SEQ) ** 0.5), 5.0, ((1, 4), (2, 8)), jnp.float32),
        "attention_output_square": jnp.clip(jnp.exp(math.log(0.23328) - 1.3862944 * jax.random.uniform(key_of[12], (LAYERS, D, D), jnp.float32) ** block_levels(key_of[12], (LAYERS, D, D), ((1, 4), (2, 8)), -0.2, 0.2)), 0.05832, 0.23328),
        "expand_weight_mean": noise(key_of[13], (LAYERS, D, FF), (0.033 * (IMAGES * SEQ) ** 0.5), 20.0, ((1, 8), (2, 4)), jnp.float32),
        "expand_weight_square": jnp.clip(jnp.exp(math.log(4.19904) - 1.3862944 * jax.random.uniform(key_of[14], (LAYERS, D, FF), jnp.float32) ** block_levels(key_of[14], (LAYERS, D, FF), ((1, 8), (2, 4)), -0.2, 0.2)), 1.04976, 4.19904),
        "reduce_weight_mean": noise(key_of[15], (LAYERS, FF, D), (0.055 * (IMAGES * SEQ) ** 0.5), 32.0, ((1, 4), (2, 8)), jnp.float32),
        "reduce_weight_square": jnp.clip(jnp.exp(math.log(11.664) - 1.3862944 * jax.random.uniform(key_of[16], (LAYERS, FF, D), jnp.float32) ** block_levels(key_of[16], (LAYERS, FF, D), ((1, 4), (2, 8)), -0.2, 0.2)), 2.916, 11.664),
        "head_bias_mean": noise(key_of[17], (LAYERS, 2, D), (0.11 * (IMAGES * SEQ) ** 0.5), 64.0, ((2, 4),), jnp.float32),
        "head_bias_square": jnp.clip(jnp.exp(math.log(46.656) - 1.3862944 * jax.random.uniform(key_of[18], (LAYERS, 2, D), jnp.float32) ** block_levels(key_of[18], (LAYERS, 2, D), ((2, 4),), -0.2, 0.2)), 11.664, 46.656),
        "expand_bias_mean": noise(key_of[19], (LAYERS, FF), (0.033 * (IMAGES * SEQ) ** 0.5), 20.0, ((1, 4),), jnp.float32),
        "expand_bias_square": jnp.clip(jnp.exp(math.log(4.19904) - 1.3862944 * jax.random.uniform(key_of[20], (LAYERS, FF), jnp.float32) ** block_levels(key_of[20], (LAYERS, FF), ((1, 4),), -0.2, 0.2)), 1.04976, 4.19904),
        "vector_params_mean": noise(key_of[21], (LAYERS, 6, D), (0.165 * (IMAGES * SEQ) ** 0.5), 112.0, ((2, 32),), jnp.float32),
        "vector_params_square": jnp.clip(jnp.exp(math.log(104.976) - 1.3862944 * jax.random.uniform(key_of[22], (LAYERS, 6, D), jnp.float32) ** block_levels(key_of[22], (LAYERS, 6, D), ((2, 32),), -0.2, 0.2)), 26.244, 104.976),
    }


norm_eps = 1e-06
masked_score = -1e+30
decay_first = 0.9
decay_second = 0.999
adam_eps = 1e-08
highest = lax.Precision.HIGHEST

@jax.custom_vjp
def low(v):
    return lax.optimization_barrier(v.astype(jnp.bfloat16)).astype(jnp.float32)

@jax.custom_vjp
def low_back(v):
    return v

def low_keep(v):
    return (low(v), None)

def low_pass(kept, grad):
    return (grad,)

def back_keep(v):
    return (v, None)

def back_low(kept, grad):
    return (low(grad),)
low.defvjp(low_keep, low_pass)
low_back.defvjp(back_keep, back_low)

def normalize(values):
    centre = lax.optimization_barrier(jnp.mean(values, axis=-1, keepdims=True))
    shifted = values - centre
    return shifted * lax.rsqrt(lax.optimization_barrier(jnp.mean(shifted * shifted, axis=-1, keepdims=True)) + norm_eps)

def attend_image(bundle):
    queries, key_rows, value_rows = bundle
    scores = low_back(jnp.einsum('qhd,khd->hqk', queries, key_rows, precision=highest))
    key_valid = jnp.arange(scores.shape[-1], dtype=jnp.int32) < SEQ
    scores = jnp.where(key_valid[None, None, :], scores, masked_score)
    weights = low(jax.nn.softmax(scores, axis=-1))
    return jnp.einsum('hqk,khd->qhd', weights, value_rows, precision=highest)

def layer_forward(stream, in_weight, out_weight, up_weight, down_weight, head_rows, expand_row, vectors):
    images, seq_rows, model_width = stream.shape
    heads_shape = (images, seq_rows, HEADS, HEAD_DIM)
    shaped = low(normalize(stream) * vectors[0] + vectors[1])
    joined = low(in_weight).reshape(model_width, 3 * model_width)
    projected = jnp.einsum('isd,dk->isk', shaped, joined, precision=highest)
    queries = low(low_back(projected[..., :model_width] + head_rows[0]) * HEAD_DIM ** (-0.5))
    key_rows = low(low_back(projected[..., model_width:2 * model_width]))
    value_rows = low(low_back(projected[..., 2 * model_width:] + head_rows[1]))
    mixture = lax.map(jax.checkpoint(attend_image), (queries.reshape(heads_shape), key_rows.reshape(heads_shape), value_rows.reshape(heads_shape)))
    mixture = low(low_back(mixture.reshape(images, seq_rows, model_width)))
    branch = low_back(jnp.einsum('isk,kd->isd', mixture, low(out_weight), precision=highest) + vectors[4])
    middle = stream + branch
    shaped_two = low(normalize(middle) * vectors[2] + vectors[3])
    hidden = low_back(jnp.einsum('isd,df->isf', shaped_two, low(up_weight), precision=highest) + expand_row)
    activated = low(jax.nn.gelu(hidden))
    branch_two = low_back(jnp.einsum('isf,fd->isd', activated, low(down_weight), precision=highest) + vectors[5])
    return middle + branch_two

def forward_all(stream, attention_input, attention_output, expand_weight, reduce_weight, head_bias, expand_bias, vector_params):
    outputs = []
    for layer_index in range(LAYERS):
        stream = layer_forward(stream, attention_input[layer_index], attention_output[layer_index], expand_weight[layer_index], reduce_weight[layer_index], head_bias[layer_index], expand_bias[layer_index], vector_params[layer_index])
        outputs.append(stream)
    return jnp.stack(outputs)

def adam_step(weight, gradient, first_moment, second, step_rate, weight_decay):
    first_new = decay_first * first_moment + (1.0 - decay_first) * gradient
    second_new = decay_second * second + (1.0 - decay_second) * gradient * gradient
    first_hat = first_new / (1.0 - decay_first ** STEP)
    second_hat = second_new / (1.0 - decay_second ** STEP)
    weight_new = weight - step_rate * (first_hat / (jnp.sqrt(second_hat) + adam_eps) + weight_decay * weight)
    return (weight_new, first_new, second_new)

def reference(stream_in, cotangent, attention_input, attention_output, expand_weight, reduce_weight, head_bias, expand_bias, vector_params, attention_input_mean, attention_input_square, attention_output_mean, attention_output_square, expand_weight_mean, expand_weight_square, reduce_weight_mean, reduce_weight_square, head_bias_mean, head_bias_square, expand_bias_mean, expand_bias_square, vector_params_mean, vector_params_square):
    activations, pullback = jax.vjp(forward_all, stream_in, attention_input, attention_output, expand_weight, reduce_weight, head_bias, expand_bias, vector_params)
    row_valid = (jnp.arange(SEQ_PAD, dtype=jnp.int32) < SEQ).astype(jnp.float32)
    last_grad = cotangent * row_valid[None, :, None]
    seeds = jnp.concatenate([jnp.zeros((LAYERS - 1,) + cotangent.shape, jnp.float32), last_grad[None]], axis=0)
    gradients = pullback(seeds)
    stream_grad = gradients[0]
    in_new, in_mean, in_square = adam_step(attention_input, gradients[1], attention_input_mean, attention_input_square, 0.03, 0.1)
    out_new, out_mean, out_square = adam_step(attention_output, gradients[2], attention_output_mean, attention_output_square, 0.3, 0.1)
    up_new, up_mean, up_square = adam_step(expand_weight, gradients[3], expand_weight_mean, expand_weight_square, 0.03, 0.1)
    down_new, down_mean, down_square = adam_step(reduce_weight, gradients[4], reduce_weight_mean, reduce_weight_square, 0.015, 0.1)
    head_new, head_mean, head_square = adam_step(head_bias, gradients[5], head_bias_mean, head_bias_square, 0.2, 0.0)
    bias_new, bias_mean, bias_square = adam_step(expand_bias, gradients[6], expand_bias_mean, expand_bias_square, 0.2, 0.0)
    vector_new, vector_mean, vector_square = adam_step(vector_params, gradients[7], vector_params_mean, vector_params_square, 0.2, 0.0)
    return (activations, stream_grad, in_new, in_mean, in_square, out_new, out_mean, out_square, up_new, up_mean, up_square, down_new, down_mean, down_square, head_new, head_mean, head_square, bias_new, bias_mean, bias_square, vector_new, vector_mean, vector_square)
```

```python
import jax
import jax.numpy as jnp
from jax import lax
from jax.experimental import pallas as pl
from jax.experimental.pallas import tpu as pltpu
from jax.sharding import Mesh, PartitionSpec as P

HEAD_DIM = 72
SEQ = 729
LAYERS = 2
STEP = 10

norm_eps = 1e-06
masked_score = -1e30
decay_first = 0.9
decay_second = 0.999
adam_eps = 1e-08

DP = ("y", "x", "core")
ALL = ("y", "x", "core", "tensor")
OWNERS = ("tensor", "y", "x", "core")
COLUMN = ("core", "tensor")


def normalize(values):
    centre = jnp.mean(values, axis=-1, keepdims=True)
    shifted = values - centre
    inverse = lax.rsqrt(jnp.mean(shifted * shifted, axis=-1, keepdims=True) + norm_eps)
    return (shifted * inverse, inverse)


def norm_back(shaped_grad, normed, inverse, gain_row):
    scaled = shaped_grad * gain_row
    centred = scaled - jnp.mean(scaled, axis=-1, keepdims=True)
    return inverse * (centred - normed * jnp.mean(scaled * normed, axis=-1, keepdims=True))


def adam_step(weight, gradient, first_moment, second, step_rate, weight_decay):
    first_new = decay_first * first_moment + (1.0 - decay_first) * gradient
    second_new = decay_second * second + (1.0 - decay_second) * gradient * gradient
    first_hat = first_new / (1.0 - decay_first**STEP)
    second_hat = second_new / (1.0 - decay_second**STEP)
    weight_new = weight - step_rate * (
        first_hat / (jnp.sqrt(second_hat) + adam_eps) + weight_decay * weight
    )
    return (weight_new, first_new, second_new)


def row_sum(values):
    return jnp.sum(values, axis=-2, dtype=jnp.float32)


def after(value, other):
    return value + (other[(0,) * other.ndim] * 0).astype(value.dtype)


class Column:
    def __init__(self, tensor_size):
        self.size = tensor_size
        self.span = tensor_size // 4
        self.members = tensor_size // 2

    def worker(self, image, chunk):
        return (chunk % 2) * self.size + image * self.span + chunk // 2

    def moves(self, turn):
        pairs = []
        for core in range(2):
            for place in range(self.size):
                image = 2 * core + (place % 2 + turn) % 2
                pairs.append((core * self.size + place, self.worker(image, place // 2)))
        return pairs

    def to_work(self, held):
        held = low(held)
        odd = lax.axis_index("tensor") % 2
        first = lax.ppermute(jnp.where(odd == 0, held[0], held[1]), COLUMN, self.moves(0))
        second = lax.ppermute(jnp.where(odd == 0, held[1], held[0]), COLUMN, self.moves(1))
        swapped = (lax.axis_index("tensor") // self.span) % 2
        return jnp.concatenate(
            [jnp.where(swapped == 0, first, second), jnp.where(swapped == 0, second, first)], axis=0
        ).astype(jnp.float32)

    def to_rest(self, worked):
        blocks = low(worked).reshape(2, worked.shape[0] // 2, worked.shape[1])
        swapped = (lax.axis_index("tensor") // self.span) % 2
        back = lambda turn: [(there, here) for here, there in self.moves(turn)]
        first = lax.ppermute(jnp.where(swapped == 0, blocks[0], blocks[1]), COLUMN, back(0))
        second = lax.ppermute(jnp.where(swapped == 0, blocks[1], blocks[0]), COLUMN, back(1))
        odd = lax.axis_index("tensor") % 2
        return jnp.stack(
            [jnp.where(odd == 0, first, second), jnp.where(odd == 0, second, first)]
        ).astype(jnp.float32)

    def chunk(self):
        return (lax.axis_index("tensor") % self.span) * 2 + lax.axis_index("core")

    def around(self, values, step):
        pairs = []
        for image in range(4):
            for here in range(self.members):
                there = (here + step) % self.members
                pairs.append((self.worker(image, here), self.worker(image, there)))
        return lax.ppermute(values, COLUMN, pairs)


def swap(value, axes, bit):
    return lax.ppermute(value, axes, [(i, i ^ bit) for i in range(lax.axis_size(axes))])


def bits_of(size):
    return [1 << k for k in range(size.bit_length() - 1)]


def gather_small(value, axes):
    index = lax.axis_index(axes)
    for bit in bits_of(lax.axis_size(axes)):
        other = swap(value, axes, bit)
        value = jnp.where(
            index & bit == 0,
            jnp.concatenate([value, other], axis=0),
            jnp.concatenate([other, value], axis=0),
        )
    return value


def sum_small(value):
    for axes in (DP, "tensor"):
        for bit in bits_of(lax.axis_size(axes)):
            value = value + swap(value, axes, bit)
    return value


class Blocks:
    def __init__(self, array, lanes, columns, shard_rows):
        self.array, self.lanes, self.columns = array, lanes, columns
        self.places, self.rows, _ = array.shape
        self.shard_rows = shard_rows
        self.matrices = len(lanes)

    def scratch(self, columns):
        return [
            pltpu.VMEM((2, self.rows, columns), jnp.bfloat16),
            pltpu.SemaphoreType.DMA((2,)),
        ]

    def stream(self, matrix, ref, buffer, sems, first=0):
        place = pl.program_id(0)
        slot = lax.rem(place, 2)
        lanes = pl.ds(self.lanes[matrix] + first, buffer.shape[2])

        def copy(place, slot):
            return pltpu.make_async_copy(
                ref.at[place, :, lanes], buffer.at[slot], sems.at[slot]
            )

        @pl.when(place == 0)
        def _():
            copy(place, slot).start()

        @pl.when(place + 1 < self.places)
        def _():
            copy(place + 1, 1 - slot).start()

        copy(place, slot).wait()
        return buffer.at[slot]


class Sums:
    def __init__(self, blocks):
        self.blocks = blocks
        count = blocks.matrices * blocks.places
        if blocks.shard_rows % 16:
            self.owners, self.block_rows = 1, blocks.rows
            self.shapes = [(count, blocks.rows, blocks.columns)]
        else:
            self.owners, self.block_rows = blocks.rows // blocks.shard_rows, blocks.shard_rows
            self.shapes = [(self.owners // 2, count, self.block_rows, blocks.columns)] * 2

    def outs(self):
        return [jax.ShapeDtypeStruct(shape, jnp.bfloat16) for shape in self.shapes]

    def scratch(self):
        blocks = self.blocks
        return [
            pltpu.VMEM((2, blocks.matrices, blocks.rows, blocks.columns), jnp.bfloat16),
            pltpu.SemaphoreType.DMA((2, blocks.matrices, self.owners)),
        ]

    def copies(self, place, slot, core, outs, buffer, sems):
        result = []
        for matrix in range(self.blocks.matrices):
            number = matrix * self.blocks.places + place
            for owner in range(self.owners):
                if self.owners == 1:
                    row, target = 0, outs[0].at[number]
                else:
                    row = pl.multiple_of((owner ^ core) * self.block_rows, 16)
                    target = outs[owner % 2].at[owner // 2, number]
                result.append(
                    pltpu.make_async_copy(
                        buffer.at[slot, matrix, pl.ds(row, self.block_rows)],
                        target,
                        sems.at[slot, matrix, owner],
                    )
                )
        return result

    def write(self, values, core, outs, buffer, sems):
        place = pl.program_id(0)
        slot = lax.rem(place, 2)

        @pl.when(place >= 2)
        def _():
            for copy in self.copies(place - 2, slot, core, outs, buffer, sems):
                copy.wait()

        for matrix, value in enumerate(values):
            value(buffer.at[slot, matrix])
        for copy in self.copies(place, slot, core, outs, buffer, sems):
            copy.start()

        @pl.when(place == self.blocks.places - 1)
        def _():
            for back in range(min(2, self.blocks.places)):
                there = lax.rem(place - back, 2)
                for copy in self.copies(place - back, there, core, outs, buffer, sems):
                    copy.wait()


def mul(left, right):
    return lax.dot_general(left, right, (((1,), (0,)), ((), ())), preferred_element_type=jnp.float32)


def mul_back(left, right):
    return lax.dot_general(left, right, (((1,), (1,)), ((), ())), preferred_element_type=jnp.float32)


def accumulate(ref, value):
    @pl.when(pl.program_id(0) == 0)
    def _():
        ref[...] = value

    @pl.when(pl.program_id(0) != 0)
    def _():
        ref[...] += value


gelu_scale = 0.7978845608028654
gelu_cubic = 0.044715


def whole_tiles(rows):
    return -(-rows // 16) * 16


def whole_block(shape):
    return pl.BlockSpec(shape, lambda place: (0,) * len(shape))


def place_block(shape):
    return pl.BlockSpec((1,) + shape[1:], lambda place: (place,) + (0,) * (len(shape) - 1))


anywhere = pl.BlockSpec(memory_space=pl.ANY)
scalar = pl.BlockSpec(memory_space=pltpu.SMEM)


def call(body, blocks, shared, placed, outs, out_specs, scratch, flops, ties=()):
    ahead = 2 + len(shared) + len(placed)
    core = lax.axis_index("core").astype(jnp.int32).reshape(1)
    return pl.pallas_call(
        lambda *refs: body(*refs[:ahead], *refs[ahead + len(ties) :]),
        grid=(blocks.places,),
        out_shape=outs,
        in_specs=[scalar]
        + [whole_block(value.shape) for value in shared]
        + [place_block(value.shape) for value in placed]
        + [anywhere] * (1 + len(ties)),
        out_specs=out_specs,
        scratch_shapes=scratch,
        compiler_params=pltpu.CompilerParams(
            dimension_semantics=("arbitrary",), vmem_limit_bytes=56 * 1024 * 1024
        ),
        cost_estimate=pl.CostEstimate(flops=flops // 16, bytes_accessed=0, transcendentals=0),
    )(core, *shared, *placed, blocks.array, *ties)


def mul_first(left, right):
    return lax.dot_general(left, right, (((0,), (0,)), ((), ())), preferred_element_type=jnp.float32)


def turned(values):
    return values.T.astype(jnp.bfloat16)


def low(values):
    return values.astype(jnp.bfloat16)


def first_step(body):
    pl.when(pl.program_id(0) == 0)(body)


def last_step(body):
    pl.when(pl.program_id(0) == pl.num_programs(0) - 1)(body)


def project_in(blocks, stream, vectors, bias, scale, ties=()):
    rows, width = stream.shape
    columns = bias.shape[2]
    taken = min(-(-columns // 128) * 128, blocks.columns)

    def body(core_ref, stream_ref, vectors_ref, scale_ref, bias_ref, *refs):
        weights, out_ref, shaped, buffer, sems = refs
        whole = blocks.stream(0, weights, buffer, sems)

        @first_step
        def _():
            normed, _ = normalize(stream_ref[...])
            shaped[...] = low(normed * vectors_ref[0:1] + vectors_ref[1:2])

        projected = mul(shaped[...], whole[...])[:, :columns]
        out_ref[0, :rows] = low((projected + bias_ref[0]) * scale_ref[...])

    shape = (blocks.places, whole_tiles(rows), columns)
    return call(
        body,
        blocks,
        [stream, vectors, scale],
        [bias],
        [jax.ShapeDtypeStruct(shape, jnp.bfloat16)],
        [place_block(shape)],
        [pltpu.VMEM((rows, width), jnp.bfloat16)] + blocks.scratch(taken),
        2 * rows * width * columns * blocks.places,
        ties,
    )[0]


def attend(blocks, stream, vectors, chunks, key_shift, ties=()):
    places, _, joined_cols = chunks[0].shape
    rows = stream.shape[0]
    columns = joined_cols // 3
    count = columns // HEAD_DIM
    members = len(chunks)
    width = blocks.rows
    first_lane = 3 * columns // 128 * 128
    skip = 3 * columns - first_lane

    def body(core_ref, stream_ref, vectors_ref, shift_ref, *refs):
        chunk_refs = refs[:members]
        weights, middle_ref, out_ref, log_ref, buffer, sems = refs[members:]
        whole = blocks.stream(0, weights, buffer, sems, first_lane)

        @first_step
        def _():
            middle_ref[...] = stream_ref[...] + vectors_ref[4:5]

        for head in range(count):
            first = head * HEAD_DIM
            query = chunk_refs[0][0, :rows, first : first + HEAD_DIM]
            scores = []
            for number, ref in enumerate(chunk_refs):
                key = ref[0, :rows, columns + first : columns + first + HEAD_DIM]
                scores.append(mul_back(key, query) + shift_ref[number])
            peak = scores[0].max(axis=0, keepdims=True)
            for score in scores[1:]:
                peak = jnp.maximum(peak, score.max(axis=0, keepdims=True))
            exponents = [jnp.exp(score - peak) for score in scores]
            total = sum(exponent.sum(axis=0, keepdims=True) for exponent in exponents)
            log_ref[0, head : head + 1] = peak + jnp.log(total)
            share = 1.0 / total
            mixed = 0.0
            for exponent, ref in zip(exponents, chunk_refs):
                value = ref[0, :rows, 2 * columns + first : 2 * columns + first + HEAD_DIM]
                mixed += mul_first(value, low(exponent * share))
            out_ref[0, :, first : first + HEAD_DIM] = turned(mixed)
        middle_ref[...] += mul_back(out_ref[0], whole[...][:, skip : skip + columns])

    return call(
        body,
        blocks,
        [stream, vectors, key_shift],
        list(chunks),
        [
            jax.ShapeDtypeStruct((rows, width), jnp.float32),
            jax.ShapeDtypeStruct((places, rows, columns), jnp.bfloat16),
            jax.ShapeDtypeStruct((places, count, rows), jnp.float32),
        ],
        [
            whole_block((rows, width)),
            place_block((places, rows, columns)),
            place_block((places, count, rows)),
        ],
        blocks.scratch(blocks.columns - first_lane),
        2 * places * rows * columns * (2 * rows * members + width),
        ties,
    )


def feed_forward(blocks, middle, vectors, bias, ties=()):
    rows, width = middle.shape

    def body(core_ref, middle_ref, vectors_ref, bias_ref, *refs):
        weights, out_ref, shaped, up_buffer, up_sems, down_buffer, down_sems = refs
        up = blocks.stream(0, weights, up_buffer, up_sems)
        down = blocks.stream(1, weights, down_buffer, down_sems)

        @first_step
        def _():
            normed, _ = normalize(middle_ref[...])
            shaped[...] = low(normed * vectors_ref[2:3] + vectors_ref[3:4])
            out_ref[...] = middle_ref[...] + vectors_ref[5:6]

        hidden = mul(shaped[...], up[...]) + bias_ref[0]
        bent = jnp.tanh(gelu_scale * (hidden + gelu_cubic * hidden * hidden * hidden))
        activated = low(0.5 * hidden * (1.0 + bent))
        out_ref[...] += mul_back(activated, down[...])

    return call(
        body,
        blocks,
        [middle, vectors],
        [bias],
        [jax.ShapeDtypeStruct((rows, width), jnp.float32)],
        [whole_block((rows, width))],
        [pltpu.VMEM((rows, width), jnp.bfloat16)] + blocks.scratch(blocks.columns) * 2,
        4 * rows * width * blocks.columns * blocks.places,
        ties,
    )[0]


def by_rows(rows):
    size = rows // 3 if rows % 48 == 0 else rows
    return [slice(first, first + size) for first in range(0, rows, size)]


def feed_forward_back(blocks, middle, vectors, grad, bias):
    rows, width = middle.shape
    sums = Sums(blocks)
    number = len(sums.shapes)

    def body(core_ref, middle_ref, vectors_ref, grad_ref, bias_ref, *refs):
        weights, out_ref, vector_out, bias_out, *refs = refs
        outs, refs = refs[:number], refs[number:]
        shaped, shaped_turned, branch, branch_turned = refs[:4]
        up_buffer, up_sems, down_buffer, down_sems, buffer, sems = refs[4:]
        up = blocks.stream(0, weights, up_buffer, up_sems)
        down = blocks.stream(1, weights, down_buffer, down_sems)

        @first_step
        def _():
            normed, _ = normalize(middle_ref[...])
            value = normed * vectors_ref[2:3] + vectors_ref[3:4]
            shaped[...] = low(value)
            shaped_turned[...] = turned(value)
            branch[...] = low(grad_ref[...])
            branch_turned[...] = turned(grad_ref[...])
            vector_out[2:3] = row_sum(branch[...].astype(jnp.float32))[None]

        hidden = mul(shaped[...], up[...]) + bias_ref[0]
        square = hidden * hidden
        bent = jnp.tanh(gelu_scale * hidden * (1.0 + gelu_cubic * square))
        half = 0.5 * (1.0 + bent)
        activated = low(hidden * half)
        slope = half + (0.5 * gelu_scale) * hidden * (1.0 - bent * bent) * (
            1.0 + (3.0 * gelu_cubic) * square
        )
        hidden_grad = low(mul(branch[...], down[...]) * slope)
        bias_out[0] = jnp.sum(hidden_grad.astype(jnp.float32), axis=0, keepdims=True)
        accumulate(out_ref, mul_back(hidden_grad, up[...]))

        def up_grad(ref):
            for part in by_rows(width):
                ref[part] = low(mul(shaped_turned[part], hidden_grad))

        def down_grad(ref):
            for part in by_rows(width):
                ref[part] = low(mul(branch_turned[part], activated))

        sums.write([up_grad, down_grad], core_ref[0], outs, buffer, sems)

        @last_step
        def _():
            normed, inverse = normalize(middle_ref[...])
            shaped_grad = out_ref[...]
            vector_out[0:1] = row_sum(shaped_grad * normed)[None]
            vector_out[1:2] = row_sum(shaped_grad)[None]
            out_ref[...] = grad_ref[...] + norm_back(
                shaped_grad, normed, inverse, vectors_ref[2:3]
            )

    return call(
        body,
        blocks,
        [middle, vectors, grad],
        [bias],
        [
            jax.ShapeDtypeStruct((rows, width), jnp.float32),
            jax.ShapeDtypeStruct((3, width), jnp.float32),
            jax.ShapeDtypeStruct(bias.shape, jnp.float32),
        ]
        + sums.outs(),
        [whole_block((rows, width)), whole_block((3, width)), place_block(bias.shape)]
        + [anywhere] * number,
        [
            pltpu.VMEM((rows, width), jnp.bfloat16),
            pltpu.VMEM((width, rows), jnp.bfloat16),
        ]
        * 2
        + blocks.scratch(blocks.columns) * 2
        + sums.scratch(),
        10 * rows * width * blocks.columns * blocks.places,
    )


def attend_back(blocks, grad, chunks, key_shift, log_total, score_scale, ties=()):
    places, _, joined_cols = chunks[0].shape
    rows = grad.shape[0]
    columns = joined_cols // 3
    count = columns // HEAD_DIM
    members = len(chunks)
    width = blocks.rows
    first_lane = 3 * columns // 128 * 128
    skip = 3 * columns - first_lane

    def body(core_ref, grad_ref, shift_ref, *refs):
        chunk_refs, log_ref, refs = refs[:members], refs[members], refs[members + 1 :]
        weights, vector_out, *refs = refs
        out_refs, (branch, mixture_grad, buffer, sems) = refs[:members], refs[members:]
        whole = blocks.stream(0, weights, buffer, sems, first_lane)

        @first_step
        def _():
            branch[...] = low(grad_ref[...])
            vector_out[...] = row_sum(branch[...].astype(jnp.float32))[None]

        mixture_grad[...] = low(mul(branch[...], whole[...])[:, skip : skip + columns])
        for out_ref in out_refs[1:]:
            out_ref[0, :rows, :columns] = jnp.zeros((rows, columns), jnp.bfloat16)
        for head in range(count):
            first = head * HEAD_DIM
            query = chunk_refs[0][0, :rows, first : first + HEAD_DIM]
            grad = mixture_grad[:, first : first + HEAD_DIM]
            log_row = log_ref[0, head : head + 1]
            weights_now, weight_grads, delta = [], [], 0.0
            for number, ref in enumerate(chunk_refs):
                key = ref[0, :rows, columns + first : columns + first + HEAD_DIM]
                value = ref[0, :rows, 2 * columns + first : 2 * columns + first + HEAD_DIM]
                weight = jnp.exp(mul_back(key, query) + shift_ref[number] - log_row)
                weight_grad = mul_back(value, grad)
                delta += (weight * weight_grad).sum(axis=0, keepdims=True)
                weights_now.append(weight)
                weight_grads.append(weight_grad)
            query_grad = 0.0
            for number, ref in enumerate(chunk_refs):
                key = ref[0, :rows, columns + first : columns + first + HEAD_DIM]
                score_grad = low(weights_now[number] * (weight_grads[number] - delta))
                value_grad = mul(low(weights_now[number]), grad)
                key_grad = mul(score_grad, query)
                query_grad += mul_first(key, score_grad)
                out_ref = out_refs[number]
                out_ref[0, :rows, columns + first : columns + first + HEAD_DIM] = low(key_grad)
                out_ref[0, :rows, 2 * columns + first : 2 * columns + first + HEAD_DIM] = low(value_grad)
            out_refs[0][0, :rows, first : first + HEAD_DIM] = turned(query_grad * score_scale)

    shape = chunks[0].shape
    return call(
        body,
        blocks,
        [grad, key_shift],
        list(chunks) + [log_total],
        [jax.ShapeDtypeStruct((1, width), jnp.float32)]
        + [jax.ShapeDtypeStruct(shape, jnp.bfloat16)] * members,
        [whole_block((1, width))] + [place_block(shape)] * members,
        [
            pltpu.VMEM((rows, width), jnp.bfloat16),
            pltpu.VMEM((rows, columns), jnp.bfloat16),
        ]
        + blocks.scratch(blocks.columns - first_lane),
        2 * places * rows * columns * (5 * rows * members + width),
        ties,
    )


def project_in_back(blocks, stream, vectors, grad, partials, mixture, ties=()):
    places, _, columns = partials[0].shape
    rows = stream.shape[0]
    width = blocks.rows
    terms = len(partials)
    sums = Sums(blocks)
    number = len(sums.shapes)
    taken = min(-(-columns // 128) * 128, blocks.columns)

    def body(core_ref, stream_ref, vectors_ref, grad_ref, *refs):
        partial_refs, mixture_ref, refs = refs[:terms], refs[terms], refs[terms + 1 :]
        weights, out_ref, vector_out, head_out, *refs = refs
        outs, refs = refs[:number], refs[number:]
        shaped_turned, branch_turned, in_buffer, in_sems, buffer, sems = refs
        whole = blocks.stream(0, weights, in_buffer, in_sems)

        @first_step
        def _():
            normed, _ = normalize(stream_ref[...])
            shaped_turned[...] = turned(normed * vectors_ref[0:1] + vectors_ref[1:2])
            branch_turned[...] = turned(grad_ref[...])

        joined = partial_refs[0][0, :rows].astype(jnp.float32)
        for ref in partial_refs[1:]:
            joined += ref[0, :rows].astype(jnp.float32)
        joined = low(joined)
        head_out[0] = jnp.sum(joined.astype(jnp.float32), axis=0, keepdims=True)
        accumulate(out_ref, mul_back(joined, whole[...][:, :columns]))

        def grads(ref):
            for part in by_rows(width):
                in_grad = mul(shaped_turned[part], joined)
                out_grad = mul(branch_turned[part], mixture_ref[0])
                ref[part] = low(fill_tiles(jnp.concatenate([in_grad, out_grad], axis=1)))

        sums.write([grads], core_ref[0], outs, buffer, sems)

        @last_step
        def _():
            normed, inverse = normalize(stream_ref[...])
            shaped_grad = out_ref[...]
            vector_out[0:1] = row_sum(shaped_grad * normed)[None]
            vector_out[1:2] = row_sum(shaped_grad)[None]
            out_ref[...] = grad_ref[...] + norm_back(
                shaped_grad, normed, inverse, vectors_ref[0:1]
            )

    head_shape = (places, 1, columns)
    return call(
        body,
        blocks,
        [stream, vectors, grad],
        list(partials) + [mixture],
        [
            jax.ShapeDtypeStruct((rows, width), jnp.float32),
            jax.ShapeDtypeStruct((2, width), jnp.float32),
            jax.ShapeDtypeStruct(head_shape, jnp.float32),
        ]
        + sums.outs(),
        [whole_block((rows, width)), whole_block((2, width)), place_block(head_shape)]
        + [anywhere] * number,
        [pltpu.VMEM((width, rows), jnp.bfloat16)] * 2 + blocks.scratch(taken) + sums.scratch(),
        2 * rows * width * (2 * columns + mixture.shape[2]) * places,
        ties,
    )


def after(value, other):
    return value + (other[(0,) * other.ndim] * 0).astype(value.dtype)


def fill_tiles(values):
    columns = values.shape[-1]
    if columns % 128 == 0:
        return values
    return jnp.pad(values, [(0, 0)] * (values.ndim - 1) + [(0, -columns % 128)])


def gather_weights(shards):
    whole = lax.all_gather(jnp.concatenate(shards, axis=1), OWNERS, axis=0, tiled=True)
    return whole.reshape(lax.axis_size("tensor"), -1, whole.shape[1])


def add_low(left, right):
    return (left.astype(jnp.float32) + right.astype(jnp.float32)).astype(jnp.bfloat16)


def scatter_grad(sides, count, rows):
    places, columns = lax.axis_size("tensor"), sides[0].shape[-1]
    if rows % 16:
        flat = sides[0].reshape(count, -1, columns)
        own = lax.psum_scatter(flat, OWNERS, scatter_dimension=1, tiled=True)
        yield own
        return own.astype(jnp.float32)
    keep, send = sides
    total = add_low(keep, swap(send, DP, 1))
    yield total
    total = lax.psum_scatter(
        total.reshape(-1, columns), ("y", "x"), scatter_dimension=0, tiled=True
    ).reshape(count, places, rows, columns)
    place = lax.axis_index("tensor")

    def part(step):
        return lax.dynamic_index_in_dim(total, (place + step) % places, axis=1, keepdims=False)

    own = part(0).astype(jnp.float32)
    for step in range(1, places):
        pairs = [(here, (here + step) % places) for here in range(places)]
        own = own + lax.ppermute(part(step), "tensor", pairs).astype(jnp.float32)
    yield own
    return own


class Scatter:
    def __init__(self, sides, count, rows):
        self.steps = scatter_grad(sides, count, rows)
        self.pending = next(self.steps)

    def total(self):
        return self.pending

    def finish(self):
        while True:
            try:
                next(self.steps)
            except StopIteration as stop:
                return stop.value


def on_device(
    stream_in,
    cotangent,
    attention_input,
    attention_output,
    expand_weight,
    reduce_weight,
    head_bias,
    expand_bias,
    vector_params,
    attention_input_mean,
    attention_input_square,
    attention_output_mean,
    attention_output_square,
    expand_weight_mean,
    expand_weight_square,
    reduce_weight_mean,
    reduce_weight_square,
    head_bias_mean,
    head_bias_square,
    expand_bias_mean,
    expand_bias_square,
    vector_params_mean,
    vector_params_square,
):
    images, block_rows, width = stream_in.shape
    places = lax.axis_size("tensor")
    column = Column(places)
    rows = images * block_rows
    members = column.members
    head_cols = head_bias.shape[2]
    score_scale = HEAD_DIM ** (-0.5)
    chunk = column.chunk()
    offsets = jnp.arange(rows, dtype=jnp.int32)
    row_valid = chunk * rows + offsets < SEQ
    key_valid = jnp.stack(
        [((chunk - step) % members) * rows + offsets < SEQ for step in range(members)]
    )
    key_shift = jnp.where(key_valid, 0.0, masked_score)[:, :, None]

    width_own = vector_params.shape[2]
    shard_rows = attention_input.shape[1]
    shards = []
    for layer in range(LAYERS):
        shards.append(
            fill_tiles(
                low(
                    jnp.concatenate(
                        [attention_input[layer].reshape(shard_rows, -1), attention_output[layer].T],
                        axis=1,
                    )
                )
            )
        )
        shards.append(fill_tiles(low(expand_weight[layer])))
        shards.append(fill_tiles(low(reduce_weight[layer].T)))
    shards[-2] = after(shards[-2], shards[0])
    early, late = gather_weights(shards[:-2]), gather_weights(shards[-2:])
    weights, lane = [], 0
    for layer in range(LAYERS):
        columns, hidden_columns = shards[3 * layer].shape[1], shards[3 * layer + 1].shape[1]
        if layer == LAYERS - 1:
            feed = Blocks(late, [0, hidden_columns], hidden_columns, shard_rows)
        else:
            first = lane + columns
            feed = Blocks(early, [first, first + hidden_columns], hidden_columns, shard_rows)
        weights.append((Blocks(early, [lane], columns, shard_rows), feed))
        lane += columns + 2 * hidden_columns

    stream = column.to_work(stream_in)
    biases = jnp.concatenate([head_bias.reshape(-1), expand_bias.reshape(-1)])
    vector_size, head_size = vector_params.size, head_bias.size
    small = jnp.concatenate([vector_params.reshape(1, -1), biases[None]], axis=1)
    small = gather_small(small, "tensor")
    vectors = gather_small(small[:, :vector_size].reshape(1, -1), DP)
    vectors = vectors.reshape(-1, LAYERS * 6, width_own)
    biases = small[:, vector_size:]
    head_rows = biases[:, :head_size].reshape(places, LAYERS, 2, head_cols)
    expand_rows = fill_tiles(biases[:, head_size:].reshape(places, LAYERS, -1))
    vectors = vectors.transpose(1, 0, 2).reshape(LAYERS, 6, width)

    zeros = jnp.zeros((places, LAYERS, head_cols), jnp.float32)
    joined_bias = jnp.concatenate([head_rows[:, :, 0], zeros, head_rows[:, :, 1]], axis=-1)
    joined_bias = joined_bias[:, :, None]
    joined_scale = jnp.where(jnp.arange(3 * head_cols) < head_cols, score_scale, 1.0)[None]
    feed_bias = [expand_rows[:, layer][:, None] for layer in range(LAYERS)]

    kept = []
    for layer in range(LAYERS):
        attention_blocks, feed_blocks = weights[layer]
        joined = project_in(
            attention_blocks,
            stream,
            vectors[layer],
            joined_bias[:, layer],
            joined_scale,
        )
        chunks = [joined] + [column.around(joined, step) for step in range(1, members)]
        middle, mixture, log_total = attend(
            attention_blocks,
            stream,
            vectors[layer],
            chunks,
            key_shift,
        )
        kept.append((stream, chunks, middle, mixture, log_total))
        if layer < LAYERS - 1:
            stream = feed_forward(feed_blocks, middle, vectors[layer], feed_bias[layer])

    grad_stream = jnp.where(row_valid[:, None], column.to_work(cotangent), 0.0)
    matrix_sums = [None] * LAYERS
    small_sums = [None] * LAYERS
    behind = []
    for layer in reversed(range(LAYERS)):
        attention_blocks, feed_blocks = weights[layer]
        stream, chunks, middle, mixture, log_total = kept[layer]
        grad_stream, feed_vectors, feed_sums, *sides = feed_forward_back(
            feed_blocks, middle, vectors[layer], grad_stream, feed_bias[layer]
        )
        feed_scatter = Scatter(sides, 2, shard_rows)
        out_vector, own, *others = attend_back(
            attention_blocks, grad_stream, chunks, key_shift, log_total, score_scale, behind
        )
        partials = [own] + [
            column.around(partial, members - step) for step, partial in enumerate(others, 1)
        ]
        grad_stream, in_vectors, head_sums, *sides = project_in_back(
            attention_blocks,
            stream,
            vectors[layer],
            grad_stream,
            partials,
            mixture,
            [feed_scatter.total()],
        )

        def fill(values):
            return jnp.pad(values[:, 0], ((0, 0), (0, small_cols - values.shape[2])))

        small_cols = max(width, head_sums.shape[2], feed_sums.shape[2])
        small = jnp.concatenate([in_vectors, feed_vectors[:2], out_vector, feed_vectors[2:]], axis=0)
        small = jnp.pad(small, ((0, 0), (0, small_cols - width)))
        small = jnp.concatenate([small, fill(head_sums), fill(feed_sums)], axis=0)
        attention_scatter = Scatter(sides, 1, shard_rows)
        behind = [attention_scatter.total()]
        small_sums[layer] = sum_small(after(small, behind[0]))
        matrix_sums[layer] = (attention_scatter, feed_scatter)

    outputs = [column.to_rest(kept[layer][0]) for layer in range(1, LAYERS)]
    last = feed_forward(weights[-1][1], kept[-1][2], vectors[-1], feed_bias[-1], behind)
    stream_grad = column.to_rest(grad_stream)
    outputs.append(column.to_rest(last))
    matrix_grads = []
    for attention_scatter, feed_scatter in matrix_sums:
        feed_grad, attention_grad = feed_scatter.finish(), attention_scatter.finish()[0]
        hidden_own = expand_weight.shape[2]
        matrix_grads.append(
            (
                attention_grad[:, : 3 * head_cols].reshape(-1, 3, head_cols),
                attention_grad[:, 3 * head_cols : 4 * head_cols].T,
                feed_grad[0, :, :hidden_own],
                feed_grad[1, :, :hidden_own].T,
            )
        )
    in_grads, out_grads, up_grads, down_grads = (
        jnp.stack([matrix_grads[layer][index] for layer in range(LAYERS)]) for index in range(4)
    )
    small_grads = jnp.stack(small_sums)
    place_index = lax.axis_index("tensor")
    vector_terms = small_grads[:, :6, :width].reshape(LAYERS, 6, -1, width_own)
    vector_grads = lax.dynamic_index_in_dim(
        vector_terms, lax.axis_index(ALL), axis=2, keepdims=False
    )
    head_grads = lax.dynamic_index_in_dim(small_grads, 6 + place_index, axis=1, keepdims=False)
    head_grads = jnp.stack(
        [head_grads[:, :head_cols], head_grads[:, 2 * head_cols : 3 * head_cols]], axis=1
    )
    bias_grads = lax.dynamic_index_in_dim(
        small_grads, 6 + places + place_index, axis=1, keepdims=False
    )[:, : expand_bias.shape[1]]
    return (
        jnp.stack(outputs),
        stream_grad,
        *adam_step(
            attention_input, in_grads, attention_input_mean, attention_input_square, 0.03, 0.1
        ),
        *adam_step(
            attention_output, out_grads, attention_output_mean, attention_output_square, 0.3, 0.1
        ),
        *adam_step(expand_weight, up_grads, expand_weight_mean, expand_weight_square, 0.03, 0.1),
        *adam_step(reduce_weight, down_grads, reduce_weight_mean, reduce_weight_square, 0.015, 0.1),
        *adam_step(head_bias, head_grads, head_bias_mean, head_bias_square, 0.2, 0.0),
        *adam_step(expand_bias, bias_grads, expand_bias_mean, expand_bias_square, 0.2, 0.0),
        *adam_step(vector_params, vector_grads, vector_params_mean, vector_params_square, 0.2, 0.0),
    )


def solution(mesh):
    dp, places = mesh.shape["dp"], mesh.shape["tensor"]
    grid = Mesh(mesh.devices.reshape(dp // 4, 2, 2, places), ALL)
    stream = P(DP, "tensor", None)
    rows_first = P(None, DP, None, "tensor")
    out_matrix = P(None, "tensor", DP)
    up_matrix = P(None, DP, "tensor")
    head = P(None, None, "tensor")
    hidden = P(None, "tensor")
    vector = P(None, None, ALL)
    kinds = (rows_first, out_matrix, up_matrix, out_matrix, head, hidden, vector)
    moments = tuple(kind for kind in kinds for _ in range(2))
    return jax.shard_map(
        on_device,
        mesh=grid,
        in_specs=(stream, stream) + kinds + moments,
        out_specs=(P(None, DP, "tensor", None), stream)
        + tuple(kind for kind in kinds for _ in range(3)),
        check_vma=False,
    )
```

```python
import jax
import jax.numpy as jnp
from jax import lax
from jax.experimental import pallas as pl
from jax.experimental.pallas import tpu as pltpu
from jax.sharding import Mesh, PartitionSpec as P

HEAD_DIM = 72
SEQ = 729
LAYERS = 2
STEP = 10

norm_eps = 1e-06
masked_score = -1e30
decay_first = 0.9
decay_second = 0.999
adam_eps = 1e-08

DP = ("y", "x", "core")
ALL = ("y", "x", "core", "tensor")
OWNERS = ("tensor", "y", "x", "core")
COLUMN = ("core", "tensor")


def normalize(values):
    centre = jnp.mean(values, axis=-1, keepdims=True)
    shifted = values - centre
    inverse = lax.rsqrt(jnp.mean(shifted * shifted, axis=-1, keepdims=True) + norm_eps)
    return (shifted * inverse, inverse)


def norm_back(shaped_grad, normed, inverse, gain_row):
    scaled = shaped_grad * gain_row
    centred = scaled - jnp.mean(scaled, axis=-1, keepdims=True)
    return inverse * (centred - normed * jnp.mean(scaled * normed, axis=-1, keepdims=True))


def adam_step(weight, gradient, first_moment, second, step_rate, weight_decay):
    first_new = decay_first * first_moment + (1.0 - decay_first) * gradient
    second_new = decay_second * second + (1.0 - decay_second) * gradient * gradient
    first_hat = first_new / (1.0 - decay_first**STEP)
    second_hat = second_new / (1.0 - decay_second**STEP)
    weight_new = weight - step_rate * (
        first_hat / (jnp.sqrt(second_hat) + adam_eps) + weight_decay * weight
    )
    return (weight_new, first_new, second_new)


def row_sum(values):
    return jnp.sum(values, axis=-2, dtype=jnp.float32)


def after(value, other):
    return value + (other[(0,) * other.ndim] * 0).astype(value.dtype)


class Column:
    def __init__(self, tensor_size):
        self.size = tensor_size
        self.span = tensor_size // 4
        self.members = tensor_size // 2

    def worker(self, image, chunk):
        return (chunk % 2) * self.size + image * self.span + chunk // 2

    def moves(self, turn):
        pairs = []
        for core in range(2):
            for place in range(self.size):
                image = 2 * core + (place % 2 + turn) % 2
                pairs.append((core * self.size + place, self.worker(image, place // 2)))
        return pairs

    def to_work(self, held):
        held = low(held)
        odd = lax.axis_index("tensor") % 2
        first = lax.ppermute(jnp.where(odd == 0, held[0], held[1]), COLUMN, self.moves(0))
        second = lax.ppermute(jnp.where(odd == 0, held[1], held[0]), COLUMN, self.moves(1))
        swapped = (lax.axis_index("tensor") // self.span) % 2
        return jnp.concatenate(
            [jnp.where(swapped == 0, first, second), jnp.where(swapped == 0, second, first)], axis=0
        ).astype(jnp.float32)

    def to_rest(self, worked):
        blocks = low(worked).reshape(2, worked.shape[0] // 2, worked.shape[1])
        swapped = (lax.axis_index("tensor") // self.span) % 2
        back = lambda turn: [(there, here) for here, there in self.moves(turn)]
        first = lax.ppermute(jnp.where(swapped == 0, blocks[0], blocks[1]), COLUMN, back(0))
        second = lax.ppermute(jnp.where(swapped == 0, blocks[1], blocks[0]), COLUMN, back(1))
        odd = lax.axis_index("tensor") % 2
        return jnp.stack(
            [jnp.where(odd == 0, first, second), jnp.where(odd == 0, second, first)]
        ).astype(jnp.float32)

    def chunk(self):
        return (lax.axis_index("tensor") % self.span) * 2 + lax.axis_index("core")

    def around(self, values, step):
        pairs = []
        for image in range(4):
            for here in range(self.members):
                there = (here + step) % self.members
                pairs.append((self.worker(image, here), self.worker(image, there)))
        return lax.ppermute(values, COLUMN, pairs)


def swap(value, axes, bit):
    return lax.ppermute(value, axes, [(i, i ^ bit) for i in range(lax.axis_size(axes))])


def bits_of(size):
    return [1 << k for k in range(size.bit_length() - 1)]


def gather_small(value, axes):
    index = lax.axis_index(axes)
    for bit in bits_of(lax.axis_size(axes)):
        other = swap(value, axes, bit)
        value = jnp.where(
            index & bit == 0,
            jnp.concatenate([value, other], axis=0),
            jnp.concatenate([other, value], axis=0),
        )
    return value


def sum_small(value):
    for axes in (DP, "tensor"):
        for bit in bits_of(lax.axis_size(axes)):
            value = value + swap(value, axes, bit)
    return value


class Blocks:
    def __init__(self, array, lanes, columns, shard_rows):
        self.array, self.lanes, self.columns = array, lanes, columns
        self.places, self.rows, _ = array.shape
        self.shard_rows = shard_rows
        self.matrices = len(lanes)

    def scratch(self, columns):
        return [
            pltpu.VMEM((2, self.rows, columns), jnp.bfloat16),
            pltpu.SemaphoreType.DMA((2,)),
        ]

    def stream(self, matrix, ref, buffer, sems, first=0):
        place = pl.program_id(0)
        slot = lax.rem(place, 2)
        lanes = pl.ds(self.lanes[matrix] + first, buffer.shape[2])

        def copy(place, slot):
            return pltpu.make_async_copy(
                ref.at[place, :, lanes], buffer.at[slot], sems.at[slot]
            )

        @pl.when(place == 0)
        def _():
            copy(place, slot).start()

        @pl.when(place + 1 < self.places)
        def _():
            copy(place + 1, 1 - slot).start()

        copy(place, slot).wait()
        return buffer.at[slot]


class Sums:
    def __init__(self, blocks):
        self.blocks = blocks
        count = blocks.matrices * blocks.places
        if blocks.shard_rows % 16:
            self.owners, self.block_rows = 1, blocks.rows
            self.shapes = [(count, blocks.rows, blocks.columns)]
        else:
            self.owners, self.block_rows = blocks.rows // blocks.shard_rows, blocks.shard_rows
            self.shapes = [(self.owners // 2, count, self.block_rows, blocks.columns)] * 2

    def outs(self):
        return [jax.ShapeDtypeStruct(shape, jnp.bfloat16) for shape in self.shapes]

    def scratch(self):
        blocks = self.blocks
        return [
            pltpu.VMEM((2, blocks.matrices, blocks.rows, blocks.columns), jnp.bfloat16),
            pltpu.SemaphoreType.DMA((2, blocks.matrices, self.owners)),
        ]

    def copies(self, place, slot, core, outs, buffer, sems):
        result = []
        for matrix in range(self.blocks.matrices):
            number = matrix * self.blocks.places + place
            for owner in range(self.owners):
                if self.owners == 1:
                    row, target = 0, outs[0].at[number]
                else:
                    row = pl.multiple_of((owner ^ core) * self.block_rows, 16)
                    target = outs[owner % 2].at[owner // 2, number]
                result.append(
                    pltpu.make_async_copy(
                        buffer.at[slot, matrix, pl.ds(row, self.block_rows)],
                        target,
                        sems.at[slot, matrix, owner],
                    )
                )
        return result

    def write(self, values, core, outs, buffer, sems):
        place = pl.program_id(0)
        slot = lax.rem(place, 2)

        @pl.when(place >= 2)
        def _():
            for copy in self.copies(place - 2, slot, core, outs, buffer, sems):
                copy.wait()

        for matrix, value in enumerate(values):
            value(buffer.at[slot, matrix])
        for copy in self.copies(place, slot, core, outs, buffer, sems):
            copy.start()

        @pl.when(place == self.blocks.places - 1)
        def _():
            for back in range(min(2, self.blocks.places)):
                there = lax.rem(place - back, 2)
                for copy in self.copies(place - back, there, core, outs, buffer, sems):
                    copy.wait()


def mul(left, right):
    return lax.dot_general(left, right, (((1,), (0,)), ((), ())), preferred_element_type=jnp.float32)


def mul_back(left, right):
    return lax.dot_general(left, right, (((1,), (1,)), ((), ())), preferred_element_type=jnp.float32)


def accumulate(ref, value):
    @pl.when(pl.program_id(0) == 0)
    def _():
        ref[...] = value

    @pl.when(pl.program_id(0) != 0)
    def _():
        ref[...] += value


gelu_scale = 0.7978845608028654
gelu_cubic = 0.044715


def whole_tiles(rows):
    return -(-rows // 16) * 16


def whole_block(shape):
    return pl.BlockSpec(shape, lambda place: (0,) * len(shape))


def place_block(shape):
    return pl.BlockSpec((1,) + shape[1:], lambda place: (place,) + (0,) * (len(shape) - 1))


anywhere = pl.BlockSpec(memory_space=pl.ANY)
scalar = pl.BlockSpec(memory_space=pltpu.SMEM)


def call(body, blocks, shared, placed, outs, out_specs, scratch, flops, ties=()):
    ahead = 2 + len(shared) + len(placed)
    core = lax.axis_index("core").astype(jnp.int32).reshape(1)
    return pl.pallas_call(
        lambda *refs: body(*refs[:ahead], *refs[ahead + len(ties) :]),
        grid=(blocks.places,),
        out_shape=outs,
        in_specs=[scalar]
        + [whole_block(value.shape) for value in shared]
        + [place_block(value.shape) for value in placed]
        + [anywhere] * (1 + len(ties)),
        out_specs=out_specs,
        scratch_shapes=scratch,
        compiler_params=pltpu.CompilerParams(
            dimension_semantics=("arbitrary",), vmem_limit_bytes=56 * 1024 * 1024
        ),
        cost_estimate=pl.CostEstimate(flops=flops // 16, bytes_accessed=0, transcendentals=0),
    )(core, *shared, *placed, blocks.array, *ties)


def mul_first(left, right):
    return lax.dot_general(left, right, (((0,), (0,)), ((), ())), preferred_element_type=jnp.float32)


def turned(values):
    return values.T.astype(jnp.bfloat16)


def low(values):
    return values.astype(jnp.bfloat16)


def first_step(body):
    pl.when(pl.program_id(0) == 0)(body)


def last_step(body):
    pl.when(pl.program_id(0) == pl.num_programs(0) - 1)(body)


def project_in(blocks, stream, vectors, bias, scale, ties=()):
    rows, width = stream.shape
    columns = bias.shape[2]
    taken = min(-(-columns // 128) * 128, blocks.columns)

    def body(core_ref, stream_ref, vectors_ref, scale_ref, bias_ref, *refs):
        weights, out_ref, shaped, buffer, sems = refs
        whole = blocks.stream(0, weights, buffer, sems)

        @first_step
        def _():
            normed, _ = normalize(stream_ref[...])
            shaped[...] = low(normed * vectors_ref[0:1] + vectors_ref[1:2])

        projected = mul(shaped[...], whole[...])[:, :columns]
        out_ref[0, :rows] = low((projected + bias_ref[0]) * scale_ref[...])

    shape = (blocks.places, whole_tiles(rows), columns)
    return call(
        body,
        blocks,
        [stream, vectors, scale],
        [bias],
        [jax.ShapeDtypeStruct(shape, jnp.bfloat16)],
        [place_block(shape)],
        [pltpu.VMEM((rows, width), jnp.bfloat16)] + blocks.scratch(taken),
        2 * rows * width * columns * blocks.places,
        ties,
    )[0]


def attend(blocks, stream, vectors, chunks, key_shift, ties=()):
    places, _, joined_cols = chunks[0].shape
    rows = stream.shape[0]
    columns = joined_cols // 3
    count = columns // HEAD_DIM
    members = len(chunks)
    width = blocks.rows
    first_lane = 3 * columns // 128 * 128
    skip = 3 * columns - first_lane

    def body(core_ref, stream_ref, vectors_ref, shift_ref, *refs):
        chunk_refs = refs[:members]
        weights, middle_ref, out_ref, log_ref, buffer, sems = refs[members:]
        whole = blocks.stream(0, weights, buffer, sems, first_lane)

        @first_step
        def _():
            middle_ref[...] = stream_ref[...] + vectors_ref[4:5]

        for head in range(count):
            first = head * HEAD_DIM
            query = chunk_refs[0][0, :rows, first : first + HEAD_DIM]
            scores = []
            for number, ref in enumerate(chunk_refs):
                key = ref[0, :rows, columns + first : columns + first + HEAD_DIM]
                scores.append(mul_back(key, query) + shift_ref[number])
            peak = scores[0].max(axis=0, keepdims=True)
            for score in scores[1:]:
                peak = jnp.maximum(peak, score.max(axis=0, keepdims=True))
            exponents = [jnp.exp(score - peak) for score in scores]
            total = sum(exponent.sum(axis=0, keepdims=True) for exponent in exponents)
            log_ref[0, head : head + 1] = peak + jnp.log(total)
            share = 1.0 / total
            mixed = 0.0
            for exponent, ref in zip(exponents, chunk_refs):
                value = ref[0, :rows, 2 * columns + first : 2 * columns + first + HEAD_DIM]
                mixed += mul_first(value, low(exponent * share))
            out_ref[0, :, first : first + HEAD_DIM] = turned(mixed)
        middle_ref[...] += mul_back(out_ref[0], whole[...][:, skip : skip + columns])

    return call(
        body,
        blocks,
        [stream, vectors, key_shift],
        list(chunks),
        [
            jax.ShapeDtypeStruct((rows, width), jnp.float32),
            jax.ShapeDtypeStruct((places, rows, columns), jnp.bfloat16),
            jax.ShapeDtypeStruct((places, count, rows), jnp.float32),
        ],
        [
            whole_block((rows, width)),
            place_block((places, rows, columns)),
            place_block((places, count, rows)),
        ],
        blocks.scratch(blocks.columns - first_lane),
        2 * places * rows * columns * (2 * rows * members + width),
        ties,
    )


def feed_forward(blocks, middle, vectors, bias, ties=()):
    rows, width = middle.shape

    def body(core_ref, middle_ref, vectors_ref, bias_ref, *refs):
        weights, out_ref, shaped, up_buffer, up_sems, down_buffer, down_sems = refs
        up = blocks.stream(0, weights, up_buffer, up_sems)
        down = blocks.stream(1, weights, down_buffer, down_sems)

        @first_step
        def _():
            normed, _ = normalize(middle_ref[...])
            shaped[...] = low(normed * vectors_ref[2:3] + vectors_ref[3:4])
            out_ref[...] = middle_ref[...] + vectors_ref[5:6]

        hidden = mul(shaped[...], up[...]) + bias_ref[0]
        bent = jnp.tanh(gelu_scale * (hidden + gelu_cubic * hidden * hidden * hidden))
        activated = low(0.5 * hidden * (1.0 + bent))
        out_ref[...] += mul_back(activated, down[...])

    return call(
        body,
        blocks,
        [middle, vectors],
        [bias],
        [jax.ShapeDtypeStruct((rows, width), jnp.float32)],
        [whole_block((rows, width))],
        [pltpu.VMEM((rows, width), jnp.bfloat16)] + blocks.scratch(blocks.columns) * 2,
        4 * rows * width * blocks.columns * blocks.places,
        ties,
    )[0]


def by_rows(rows):
    size = rows // 3 if rows % 48 == 0 else rows
    return [slice(first, first + size) for first in range(0, rows, size)]


def feed_forward_back(blocks, middle, vectors, grad, bias):
    rows, width = middle.shape
    sums = Sums(blocks)
    number = len(sums.shapes)

    def body(core_ref, middle_ref, vectors_ref, grad_ref, bias_ref, *refs):
        weights, out_ref, vector_out, bias_out, *refs = refs
        outs, refs = refs[:number], refs[number:]
        shaped, shaped_turned, branch, branch_turned = refs[:4]
        up_buffer, up_sems, down_buffer, down_sems, buffer, sems = refs[4:]
        up = blocks.stream(0, weights, up_buffer, up_sems)
        down = blocks.stream(1, weights, down_buffer, down_sems)

        @first_step
        def _():
            normed, _ = normalize(middle_ref[...])
            value = normed * vectors_ref[2:3] + vectors_ref[3:4]
            shaped[...] = low(value)
            shaped_turned[...] = turned(value)
            branch[...] = low(grad_ref[...])
            branch_turned[...] = turned(grad_ref[...])
            vector_out[2:3] = row_sum(branch[...].astype(jnp.float32))[None]

        hidden = mul(shaped[...], up[...]) + bias_ref[0]
        square = hidden * hidden
        bent = jnp.tanh(gelu_scale * hidden * (1.0 + gelu_cubic * square))
        half = 0.5 * (1.0 + bent)
        activated = low(hidden * half)
        slope = half + (0.5 * gelu_scale) * hidden * (1.0 - bent * bent) * (
            1.0 + (3.0 * gelu_cubic) * square
        )
        hidden_grad = low(mul(branch[...], down[...]) * slope)
        bias_out[0] = jnp.sum(hidden_grad.astype(jnp.float32), axis=0, keepdims=True)
        accumulate(out_ref, mul_back(hidden_grad, up[...]))

        def up_grad(ref):
            for part in by_rows(width):
                ref[part] = low(mul(shaped_turned[part], hidden_grad))

        def down_grad(ref):
            for part in by_rows(width):
                ref[part] = low(mul(branch_turned[part], activated))

        sums.write([up_grad, down_grad], core_ref[0], outs, buffer, sems)

        @last_step
        def _():
            normed, inverse = normalize(middle_ref[...])
            shaped_grad = out_ref[...]
            vector_out[0:1] = row_sum(shaped_grad * normed)[None]
            vector_out[1:2] = row_sum(shaped_grad)[None]
            out_ref[...] = grad_ref[...] + norm_back(
                shaped_grad, normed, inverse, vectors_ref[2:3]
            )

    return call(
        body,
        blocks,
        [middle, vectors, grad],
        [bias],
        [
            jax.ShapeDtypeStruct((rows, width), jnp.float32),
            jax.ShapeDtypeStruct((3, width), jnp.float32),
            jax.ShapeDtypeStruct(bias.shape, jnp.float32),
        ]
        + sums.outs(),
        [whole_block((rows, width)), whole_block((3, width)), place_block(bias.shape)]
        + [anywhere] * number,
        [
            pltpu.VMEM((rows, width), jnp.bfloat16),
            pltpu.VMEM((width, rows), jnp.bfloat16),
        ]
        * 2
        + blocks.scratch(blocks.columns) * 2
        + sums.scratch(),
        10 * rows * width * blocks.columns * blocks.places,
    )


def attend_back(blocks, grad, chunks, key_shift, log_total, score_scale, ties=()):
    places, _, joined_cols = chunks[0].shape
    rows = grad.shape[0]
    columns = joined_cols // 3
    count = columns // HEAD_DIM
    members = len(chunks)
    width = blocks.rows
    first_lane = 3 * columns // 128 * 128
    skip = 3 * columns - first_lane

    def body(core_ref, grad_ref, shift_ref, *refs):
        chunk_refs, log_ref, refs = refs[:members], refs[members], refs[members + 1 :]
        weights, vector_out, *refs = refs
        out_refs, (branch, mixture_grad, buffer, sems) = refs[:members], refs[members:]
        whole = blocks.stream(0, weights, buffer, sems, first_lane)

        @first_step
        def _():
            branch[...] = low(grad_ref[...])
            vector_out[...] = row_sum(branch[...].astype(jnp.float32))[None]

        mixture_grad[...] = low(mul(branch[...], whole[...])[:, skip : skip + columns])
        for out_ref in out_refs[1:]:
            out_ref[0, :rows, :columns] = jnp.zeros((rows, columns), jnp.bfloat16)
        for head in range(count):
            first = head * HEAD_DIM
            query = chunk_refs[0][0, :rows, first : first + HEAD_DIM]
            grad = mixture_grad[:, first : first + HEAD_DIM]
            log_row = log_ref[0, head : head + 1]
            weights_now, weight_grads, delta = [], [], 0.0
            for number, ref in enumerate(chunk_refs):
                key = ref[0, :rows, columns + first : columns + first + HEAD_DIM]
                value = ref[0, :rows, 2 * columns + first : 2 * columns + first + HEAD_DIM]
                weight = jnp.exp(mul_back(key, query) + shift_ref[number] - log_row)
                weight_grad = mul_back(value, grad)
                delta += (weight * weight_grad).sum(axis=0, keepdims=True)
                weights_now.append(weight)
                weight_grads.append(weight_grad)
            query_grad = 0.0
            for number, ref in enumerate(chunk_refs):
                key = ref[0, :rows, columns + first : columns + first + HEAD_DIM]
                score_grad = low(weights_now[number] * (weight_grads[number] - delta))
                value_grad = mul(low(weights_now[number]), grad)
                key_grad = mul(score_grad, query)
                query_grad += mul_first(key, score_grad)
                out_ref = out_refs[number]
                out_ref[0, :rows, columns + first : columns + first + HEAD_DIM] = low(key_grad)
                out_ref[0, :rows, 2 * columns + first : 2 * columns + first + HEAD_DIM] = low(value_grad)
            out_refs[0][0, :rows, first : first + HEAD_DIM] = turned(query_grad * score_scale)

    shape = chunks[0].shape
    return call(
        body,
        blocks,
        [grad, key_shift],
        list(chunks) + [log_total],
        [jax.ShapeDtypeStruct((1, width), jnp.float32)]
        + [jax.ShapeDtypeStruct(shape, jnp.bfloat16)] * members,
        [whole_block((1, width))] + [place_block(shape)] * members,
        [
            pltpu.VMEM((rows, width), jnp.bfloat16),
            pltpu.VMEM((rows, columns), jnp.bfloat16),
        ]
        + blocks.scratch(blocks.columns - first_lane),
        2 * places * rows * columns * (5 * rows * members + width),
        ties,
    )


def project_in_back(blocks, stream, vectors, grad, partials, mixture, ties=()):
    places, _, columns = partials[0].shape
    rows = stream.shape[0]
    width = blocks.rows
    terms = len(partials)
    sums = Sums(blocks)
    number = len(sums.shapes)
    taken = min(-(-columns // 128) * 128, blocks.columns)

    def body(core_ref, stream_ref, vectors_ref, grad_ref, *refs):
        partial_refs, mixture_ref, refs = refs[:terms], refs[terms], refs[terms + 1 :]
        weights, out_ref, vector_out, head_out, *refs = refs
        outs, refs = refs[:number], refs[number:]
        shaped_turned, branch_turned, in_buffer, in_sems, buffer, sems = refs
        whole = blocks.stream(0, weights, in_buffer, in_sems)

        @first_step
        def _():
            normed, _ = normalize(stream_ref[...])
            shaped_turned[...] = turned(normed * vectors_ref[0:1] + vectors_ref[1:2])
            branch_turned[...] = turned(grad_ref[...])

        joined = partial_refs[0][0, :rows].astype(jnp.float32)
        for ref in partial_refs[1:]:
            joined += ref[0, :rows].astype(jnp.float32)
        joined = low(joined)
        head_out[0] = jnp.sum(joined.astype(jnp.float32), axis=0, keepdims=True)
        accumulate(out_ref, mul_back(joined, whole[...][:, :columns]))

        def grads(ref):
            for part in by_rows(width):
                in_grad = mul(shaped_turned[part], joined)
                out_grad = mul(branch_turned[part], mixture_ref[0])
                ref[part] = low(fill_tiles(jnp.concatenate([in_grad, out_grad], axis=1)))

        sums.write([grads], core_ref[0], outs, buffer, sems)

        @last_step
        def _():
            normed, inverse = normalize(stream_ref[...])
            shaped_grad = out_ref[...]
            vector_out[0:1] = row_sum(shaped_grad * normed)[None]
            vector_out[1:2] = row_sum(shaped_grad)[None]
            out_ref[...] = grad_ref[...] + norm_back(
                shaped_grad, normed, inverse, vectors_ref[0:1]
            )

    head_shape = (places, 1, columns)
    return call(
        body,
        blocks,
        [stream, vectors, grad],
        list(partials) + [mixture],
        [
            jax.ShapeDtypeStruct((rows, width), jnp.float32),
            jax.ShapeDtypeStruct((2, width), jnp.float32),
            jax.ShapeDtypeStruct(head_shape, jnp.float32),
        ]
        + sums.outs(),
        [whole_block((rows, width)), whole_block((2, width)), place_block(head_shape)]
        + [anywhere] * number,
        [pltpu.VMEM((width, rows), jnp.bfloat16)] * 2 + blocks.scratch(taken) + sums.scratch(),
        2 * rows * width * (2 * columns + mixture.shape[2]) * places,
        ties,
    )


def after(value, other):
    return value + (other[(0,) * other.ndim] * 0).astype(value.dtype)


def fill_tiles(values):
    columns = values.shape[-1]
    if columns % 128 == 0:
        return values
    return jnp.pad(values, [(0, 0)] * (values.ndim - 1) + [(0, -columns % 128)])


def gather_weights(shards):
    whole = lax.all_gather(jnp.concatenate(shards, axis=1), OWNERS, axis=0, tiled=True)
    return whole.reshape(lax.axis_size("tensor"), -1, whole.shape[1])


def add_low(left, right):
    return (left.astype(jnp.float32) + right.astype(jnp.float32)).astype(jnp.bfloat16)


def scatter_grad(sides, count, rows, ahead=None):
    places, columns = lax.axis_size("tensor"), sides[0].shape[-1]
    if rows % 16:
        flat = sides[0].reshape(count, -1, columns)
        own = lax.psum_scatter(flat, OWNERS, scatter_dimension=1, tiled=True)
        yield own
        return own.astype(jnp.float32)
    keep, send = sides
    total = add_low(keep, swap(send, DP, 1))
    yield total
    total = lax.psum_scatter(
        total.reshape(-1, columns), ("y", "x"), scatter_dimension=0, tiled=True
    ).reshape(count, places, rows, columns)
    yield total
    if ahead is not None:
        total = after(total, ahead.given_by(2))
    place = lax.axis_index("tensor")

    def part(step):
        return lax.dynamic_index_in_dim(total, (place + step) % places, axis=1, keepdims=False)

    own = part(0).astype(jnp.float32)
    for step in range(1, places):
        pairs = [(here, (here + step) % places) for here in range(places)]
        own = own + lax.ppermute(part(step), "tensor", pairs).astype(jnp.float32)
    yield own
    return own


class Scatter:
    def __init__(self, sides, count, rows, ahead=None):
        self.steps = scatter_grad(sides, count, rows, ahead)
        self.given, self.result = [next(self.steps)], None

    def given_by(self, step):
        while len(self.given) <= step:
            try:
                self.given.append(next(self.steps))
            except StopIteration as stop:
                self.result = self.result if stop.value is None else stop.value
                self.given.append(self.given[-1])
        return self.given[step]

    def finish(self):
        self.given_by(4)
        return self.result


def on_device(
    stream_in,
    cotangent,
    attention_input,
    attention_output,
    expand_weight,
    reduce_weight,
    head_bias,
    expand_bias,
    vector_params,
    attention_input_mean,
    attention_input_square,
    attention_output_mean,
    attention_output_square,
    expand_weight_mean,
    expand_weight_square,
    reduce_weight_mean,
    reduce_weight_square,
    head_bias_mean,
    head_bias_square,
    expand_bias_mean,
    expand_bias_square,
    vector_params_mean,
    vector_params_square,
):
    images, block_rows, width = stream_in.shape
    places = lax.axis_size("tensor")
    column = Column(places)
    rows = images * block_rows
    members = column.members
    head_cols = head_bias.shape[2]
    score_scale = HEAD_DIM ** (-0.5)
    chunk = column.chunk()
    offsets = jnp.arange(rows, dtype=jnp.int32)
    row_valid = chunk * rows + offsets < SEQ
    key_valid = jnp.stack(
        [((chunk - step) % members) * rows + offsets < SEQ for step in range(members)]
    )
    key_shift = jnp.where(key_valid, 0.0, masked_score)[:, :, None]

    width_own = vector_params.shape[2]
    shard_rows = attention_input.shape[1]
    shards = []
    for layer in range(LAYERS):
        shards.append(
            fill_tiles(
                low(
                    jnp.concatenate(
                        [attention_input[layer].reshape(shard_rows, -1), attention_output[layer].T],
                        axis=1,
                    )
                )
            )
        )
        shards.append(fill_tiles(low(expand_weight[layer])))
        shards.append(fill_tiles(low(reduce_weight[layer].T)))
    shards[-2] = after(shards[-2], shards[0])
    early, late = gather_weights(shards[:-2]), gather_weights(shards[-2:])
    weights, lane = [], 0
    for layer in range(LAYERS):
        columns, hidden_columns = shards[3 * layer].shape[1], shards[3 * layer + 1].shape[1]
        if layer == LAYERS - 1:
            feed = Blocks(late, [0, hidden_columns], hidden_columns, shard_rows)
        else:
            first = lane + columns
            feed = Blocks(early, [first, first + hidden_columns], hidden_columns, shard_rows)
        weights.append((Blocks(early, [lane], columns, shard_rows), feed))
        lane += columns + 2 * hidden_columns

    stream = column.to_work(stream_in)
    grad_stream = jnp.where(row_valid[:, None], column.to_work(cotangent), 0.0)
    biases = jnp.concatenate([head_bias.reshape(-1), expand_bias.reshape(-1)])
    vector_size, head_size = vector_params.size, head_bias.size
    small = jnp.concatenate([vector_params.reshape(1, -1), biases[None]], axis=1)
    small = gather_small(small, "tensor")
    vectors = gather_small(small[:, :vector_size].reshape(1, -1), DP)
    vectors = vectors.reshape(-1, LAYERS * 6, width_own)
    biases = small[:, vector_size:]
    head_rows = biases[:, :head_size].reshape(places, LAYERS, 2, head_cols)
    expand_rows = fill_tiles(biases[:, head_size:].reshape(places, LAYERS, -1))
    vectors = vectors.transpose(1, 0, 2).reshape(LAYERS, 6, width)

    zeros = jnp.zeros((places, LAYERS, head_cols), jnp.float32)
    joined_bias = jnp.concatenate([head_rows[:, :, 0], zeros, head_rows[:, :, 1]], axis=-1)
    joined_bias = joined_bias[:, :, None]
    joined_scale = jnp.where(jnp.arange(3 * head_cols) < head_cols, score_scale, 1.0)[None]
    feed_bias = [expand_rows[:, layer][:, None] for layer in range(LAYERS)]

    kept = []
    for layer in range(LAYERS):
        attention_blocks, feed_blocks = weights[layer]
        joined = project_in(
            attention_blocks,
            stream,
            vectors[layer],
            joined_bias[:, layer],
            joined_scale,
            [grad_stream] if layer == 0 else [],
        )
        chunks = [joined] + [column.around(joined, step) for step in range(1, members)]
        middle, mixture, log_total = attend(
            attention_blocks,
            stream,
            vectors[layer],
            chunks,
            key_shift,
        )
        kept.append((stream, chunks, middle, mixture, log_total))
        if layer < LAYERS - 1:
            stream = feed_forward(feed_blocks, middle, vectors[layer], feed_bias[layer])

    matrix_sums = [None] * LAYERS
    small_sums = [None] * LAYERS
    behind, ahead = [], None
    for layer in reversed(range(LAYERS)):
        attention_blocks, feed_blocks = weights[layer]
        stream, chunks, middle, mixture, log_total = kept[layer]
        grad_stream, feed_vectors, feed_sums, *sides = feed_forward_back(
            feed_blocks, middle, vectors[layer], grad_stream, feed_bias[layer]
        )
        feed_scatter = Scatter(sides, 2, shard_rows, ahead)
        out_vector, own, *others = attend_back(
            attention_blocks, grad_stream, chunks, key_shift, log_total, score_scale, behind
        )
        partials = [own] + [
            column.around(partial, members - step) for step, partial in enumerate(others, 1)
        ]
        ties = [feed_scatter.given_by(0)]
        if layer == LAYERS - 1:
            outputs = [
                column.to_rest(after(kept[number][0], grad_stream)) for number in range(1, LAYERS)
            ]
            ties = ties + outputs
        grad_stream, in_vectors, head_sums, *sides = project_in_back(
            attention_blocks,
            stream,
            vectors[layer],
            grad_stream,
            partials,
            mixture,
            ties,
        )

        def fill(values):
            return jnp.pad(values[:, 0], ((0, 0), (0, small_cols - values.shape[2])))

        small_cols = max(width, head_sums.shape[2], feed_sums.shape[2])
        small = jnp.concatenate([in_vectors, feed_vectors[:2], out_vector, feed_vectors[2:]], axis=0)
        small = jnp.pad(small, ((0, 0), (0, small_cols - width)))
        small = jnp.concatenate([small, fill(head_sums), fill(feed_sums)], axis=0)
        ahead = attention_scatter = Scatter(sides, 1, shard_rows, feed_scatter)
        behind = [attention_scatter.given_by(0)]
        small_sums[layer] = small
        matrix_sums[layer] = (attention_scatter, feed_scatter)

    attention_last, feed_last = (scatter.given_by(2) for scatter in matrix_sums[-1])
    last = feed_forward(
        weights[-1][1], kept[-1][2], vectors[-1], feed_bias[-1], behind + [feed_last]
    )
    last = after(last, attention_last)
    stream_grad = column.to_rest(after(grad_stream, attention_last))
    small_grads = sum_small(after(jnp.stack(small_sums), attention_last))
    outputs.append(column.to_rest(last))
    matrix_grads = []
    for attention_scatter, feed_scatter in matrix_sums:
        feed_grad, attention_grad = feed_scatter.finish(), attention_scatter.finish()[0]
        hidden_own = expand_weight.shape[2]
        matrix_grads.append(
            (
                attention_grad[:, : 3 * head_cols].reshape(-1, 3, head_cols),
                attention_grad[:, 3 * head_cols : 4 * head_cols].T,
                feed_grad[0, :, :hidden_own],
                feed_grad[1, :, :hidden_own].T,
            )
        )
    in_grads, out_grads, up_grads, down_grads = (
        jnp.stack([matrix_grads[layer][index] for layer in range(LAYERS)]) for index in range(4)
    )
    place_index = lax.axis_index("tensor")
    vector_terms = small_grads[:, :6, :width].reshape(LAYERS, 6, -1, width_own)
    vector_grads = lax.dynamic_index_in_dim(
        vector_terms, lax.axis_index(ALL), axis=2, keepdims=False
    )
    head_grads = lax.dynamic_index_in_dim(small_grads, 6 + place_index, axis=1, keepdims=False)
    head_grads = jnp.stack(
        [head_grads[:, :head_cols], head_grads[:, 2 * head_cols : 3 * head_cols]], axis=1
    )
    bias_grads = lax.dynamic_index_in_dim(
        small_grads, 6 + places + place_index, axis=1, keepdims=False
    )[:, : expand_bias.shape[1]]
    return (
        jnp.stack(outputs),
        stream_grad,
        *adam_step(
            attention_input, in_grads, attention_input_mean, attention_input_square, 0.03, 0.1
        ),
        *adam_step(
            attention_output, out_grads, attention_output_mean, attention_output_square, 0.3, 0.1
        ),
        *adam_step(expand_weight, up_grads, expand_weight_mean, expand_weight_square, 0.03, 0.1),
        *adam_step(reduce_weight, down_grads, reduce_weight_mean, reduce_weight_square, 0.015, 0.1),
        *adam_step(head_bias, head_grads, head_bias_mean, head_bias_square, 0.2, 0.0),
        *adam_step(expand_bias, bias_grads, expand_bias_mean, expand_bias_square, 0.2, 0.0),
        *adam_step(vector_params, vector_grads, vector_params_mean, vector_params_square, 0.2, 0.0),
    )


def solution(mesh):
    dp, places = mesh.shape["dp"], mesh.shape["tensor"]
    grid = Mesh(mesh.devices.reshape(dp // 4, 2, 2, places), ALL)
    stream = P(DP, "tensor", None)
    rows_first = P(None, DP, None, "tensor")
    out_matrix = P(None, "tensor", DP)
    up_matrix = P(None, DP, "tensor")
    head = P(None, None, "tensor")
    hidden = P(None, "tensor")
    vector = P(None, None, ALL)
    kinds = (rows_first, out_matrix, up_matrix, out_matrix, head, hidden, vector)
    moments = tuple(kind for kind in kinds for _ in range(2))
    return jax.shard_map(
        on_device,
        mesh=grid,
        in_specs=(stream, stream) + kinds + moments,
        out_specs=(P(None, DP, "tensor", None), stream)
        + tuple(kind for kind in kinds for _ in range(3)),
        check_vma=False,
    )
```
